32 devices in a mesh: wide: 16 (over z, x, core), narrow: 2 (over y).
Axes of the slice: x: 2, y: 2, z: 4, core: 2. Of those that a mesh axis runs over, the one named last changes fastest.
Arguments:
- tokens: bfloat16 [1344, 4096], P('wide'), may hold values from -16 to 16
- w_query: bfloat16 [4096, 4096], P('wide', 'narrow'), may hold values from -0.09375 to 0.09375
- w_keyvalue: bfloat16 [4096, 2, 1024], P('wide', None, 'narrow'), may hold values from -0.09375 to 0.09375
- adapter_down: bfloat16 [16, 4096, 2, 512], P('wide', None, None, 'narrow'), may hold values from -0.09375 to 0.09375
- adapter_up_query: bfloat16 [16, 512, 4096], P('wide', None, 'narrow'), may hold values from -0.25 to 0.25
- adapter_up_value: bfloat16 [16, 512, 1024], P('wide', None, 'narrow'), may hold values from -0.25 to 0.25
- request_adapter: int32 [96], P('wide'), may hold values from 0 to 15, as said below
- request_tokens: int32 [96], P('wide'), may hold values from 1 to 14, as said below
- adapter_owner: int32 [16], replicated, may hold values from 0 to 15, each once
Outputs:
- attended: bfloat16 [1344, 4096], P('wide', 'narrow')
The draws below stay inside these ranges and needn't reach their ends.
Inputs may be any that keep to these rules, and one draw needn't show every extreme that they name: `request_adapter`: the 6 requests of one index of wide name distinct adapters. At most 12 requests name one adapter, and some adapter is named by exactly 12. `request_tokens`: A request's live tokens are the first rows of its slot; each index of wide holds a request with exactly 14. Adapter a's maps are entry adapter_owner[a] of the adapter arrays.
All inputs are finite; a program needn't handle non-finite values.
Results may differ from the reference program's by a relative error of at most 0.012.
Values may be sent and summed in bfloat16 or wider, within the bound.
No kernel may reach another device: no remote copies, remote signals or barrier semaphores. Data moves between devices by JAX's collectives and lax.ppermute only.
A program may use at most 128 MiB of HBM per device.

```python
import math
import jax
import jax.numpy as jnp
from jax import lax

D = 4096
HEADS = 32
KV_HEADS = 8
HD = 128
RANK = 512
REQ_LEN = 14
REQ_DEV = 6
ADAPTERS = 16
TOKENS = 1344
REQUESTS = 96


def draw_tokens(key, part):
    key = jax.random.fold_in(key, 11)
    key_values = jax.random.fold_in(key, 0)
    values = jnp.clip(jax.random.normal(key_values, (TOKENS, D), jnp.float32), -6.0, 6.0)
    return values.astype(jnp.bfloat16)


def shuffle_one(subkey):
    return jax.random.permutation(subkey, REQ_DEV)


def draw_request_adapter(key, part):
    key = jax.random.fold_in(key, 23)
    key_order, key_spread, key_shuffle = jax.random.split(key, 3)
    adapter_order = jax.random.permutation(key_order, ADAPTERS)
    spread = jax.random.permutation(key_spread, ADAPTERS)
    half_count = REQ_DEV // 2
    quarter = ADAPTERS // 4
    step_list = jnp.arange(half_count, dtype=jnp.int32)[None, :]
    hot_slots = (spread[:, None] + step_list) % quarter
    cold_slots = quarter + (spread[:, None] + step_list) % (ADAPTERS - quarter)
    chosen_ids = adapter_order[jnp.concatenate([hot_slots, cold_slots], axis=1)]
    shuffles = jax.vmap(shuffle_one)(jax.random.split(key_shuffle, ADAPTERS))
    chosen_ids = jnp.take_along_axis(chosen_ids, shuffles, axis=1)
    return chosen_ids.reshape(REQUESTS).astype(jnp.int32)


def draw_request_tokens(key, part):
    key = jax.random.fold_in(key, 37)
    key_count, key_full = jax.random.split(key)
    counts = jax.random.randint(key_count, (REQUESTS,), 1, REQ_LEN + 1, dtype=jnp.int32)
    full_slot = jax.random.randint(key_full, (REQUESTS // REQ_DEV, 1), 0, REQ_DEV, dtype=jnp.int32)
    filled = (jnp.arange(REQ_DEV, dtype=jnp.int32)[None, :] == full_slot).reshape(REQUESTS)
    return jnp.where(filled, REQ_LEN, counts).astype(jnp.int32)


def block_scale(key, dims, cuts, smallest, largest):
    factor_of = 1.0
    for dim, shards_of in cuts:
        heights = jax.random.uniform(jax.random.fold_in(jax.random.fold_in(key, 6), dim), (shards_of,), jnp.float32, smallest / len(cuts), largest / len(cuts))
        factor_of = factor_of * jnp.repeat(jnp.exp(heights), dims[dim] // shards_of).reshape((-1,) + (1,) * (len(dims) - 1 - dim))
    return factor_of


def centred(rng, shape, scale, limit, shards=(), kind=jnp.bfloat16):
    factor_of = block_scale(rng, shape, shards, -0.22, 0.18) if shards else 1.0
    values = jax.random.normal(rng, shape, jnp.float32) * scale * factor_of
    return jnp.minimum(jnp.maximum(values, -limit), limit).astype(kind)


def setup_inputs(seed: int = 0) -> dict:
    keys = jax.random.split(jax.random.key(seed), 10)
    return {
        "tokens": draw_tokens(jax.random.fold_in(keys[9], 71), 0),
        "w_query": centred(keys[1], (D, HEADS * HD), D ** -0.5, 0.09375, ((0, 16), (1, 2))),
        "w_keyvalue": centred(keys[2], (D, 2, KV_HEADS * HD), D ** -0.5, 0.09375, ((0, 16), (2, 2))),
        "adapter_down": centred(keys[3], (ADAPTERS, D, 2, RANK), D ** -0.5, 0.09375, ((0, 16), (3, 2))),
        "adapter_up_query": centred(keys[4], (ADAPTERS, RANK, HEADS * HD), RANK ** -0.5, 0.25, ((0, 16), (2, 2))),
        "adapter_up_value": centred(keys[5], (ADAPTERS, RANK, KV_HEADS * HD), RANK ** -0.5, 0.25, ((0, 16), (2, 2))),
        "request_adapter": draw_request_adapter(jax.random.fold_in(keys[9], 71), 0),
        "request_tokens": draw_request_tokens(jax.random.fold_in(keys[9], 71), 0),
        "adapter_owner": jax.random.permutation(keys[8], ADAPTERS).astype(jnp.int32),
    }


rope_theta = 500000.0

def rope_tables(length, head_size):
    half_size = head_size // 2
    exponent = jnp.arange(half_size, dtype=jnp.float32) * (2.0 / head_size)
    frequency = rope_theta ** (-exponent)
    angles = jnp.arange(length, dtype=jnp.float32)[:, None] * frequency[None, :]
    angles = jnp.concatenate([angles, angles], axis=1)
    return (jnp.cos(angles), jnp.sin(angles))

def rotate(values, cosine, sine_table):
    half_size = values.shape[-1] // 2
    turned = jnp.concatenate([-values[..., half_size:], values[..., :half_size]], axis=-1)
    return values * cosine[:, None, :] + turned * sine_table[:, None, :]

def attend(queries, key_rows, value_rows, counts):
    length = queries.shape[1]
    scores = jnp.einsum('rikgd,rjkd->rkgij', queries.astype(jnp.float32), key_rows.astype(jnp.float32))
    scores = scores * (1.0 / math.sqrt(queries.shape[-1]))
    position = jnp.arange(length, dtype=jnp.int32)
    causal = position[None, :] <= position[:, None]
    allowed = causal[None, :, :] & (position[None, None, :] < counts[:, None, None])
    scores = jnp.where(allowed[:, None, None, :, :], scores, -1e+30)
    row_max = lax.optimization_barrier(jnp.max(scores, axis=-1, keepdims=True))
    numerators = jnp.exp(scores - row_max)
    probabilities = (numerators / lax.optimization_barrier(jnp.sum(numerators, axis=-1, keepdims=True))).astype(jnp.bfloat16)
    mixture = jnp.einsum('rkgij,rjkd->rikgd', probabilities.astype(jnp.float32), value_rows.astype(jnp.float32))
    live_rows = position[None, :] < counts[:, None]
    mixture = jnp.where(live_rows[:, :, None, None, None], mixture, 0.0)
    return mixture.astype(jnp.bfloat16)

def reference(tokens, w_query, w_keyvalue, adapter_down, adapter_up_query, adapter_up_value, request_adapter, request_tokens, adapter_owner):
    query_cols = HEADS * HD
    key_cols = KV_HEADS * HD
    group_size = HEADS // KV_HEADS
    cosine, sine_table = rope_tables(REQ_LEN, HD)
    w_both = w_keyvalue.reshape(D, 2 * key_cols)
    homes = TOKENS // (REQ_DEV * REQ_LEN)

    def one_home(inputs):
        home_rows, adapters_home, counts_home = inputs
        flat_rows = home_rows.reshape(REQ_DEV * REQ_LEN, D)
        query_base = jnp.dot(flat_rows, w_query, preferred_element_type=jnp.float32)
        keyvalue_base = jnp.dot(flat_rows, w_both, preferred_element_type=jnp.float32)
        owners = adapter_owner[adapters_home]
        down_maps = adapter_down[owners].astype(jnp.float32)
        shrunk = jnp.einsum('rld,rdkq->rlkq', home_rows.astype(jnp.float32), down_maps).astype(jnp.bfloat16)
        up_query = adapter_up_query[owners].astype(jnp.float32)
        up_value = adapter_up_value[owners].astype(jnp.float32)
        delta_query = jnp.einsum('rlq,rqc->rlc', shrunk[:, :, 0].astype(jnp.float32), up_query).astype(jnp.bfloat16)
        delta_value = jnp.einsum('rlq,rqc->rlc', shrunk[:, :, 1].astype(jnp.float32), up_value).astype(jnp.bfloat16)
        queries = query_base.reshape(REQ_DEV, REQ_LEN, query_cols) + delta_query.astype(jnp.float32)
        queries = rotate(queries.reshape(REQ_DEV, REQ_LEN, HEADS, HD), cosine, sine_table).astype(jnp.bfloat16)
        key_rows = rotate(keyvalue_base[:, :key_cols].reshape(REQ_DEV, REQ_LEN, KV_HEADS, HD), cosine, sine_table).astype(jnp.bfloat16)
        value_rows = keyvalue_base[:, key_cols:].reshape(REQ_DEV, REQ_LEN, key_cols) + delta_value.astype(jnp.float32)
        value_rows = value_rows.reshape(REQ_DEV, REQ_LEN, KV_HEADS, HD).astype(jnp.bfloat16)
        result = attend(queries.reshape(REQ_DEV, REQ_LEN, KV_HEADS, group_size, HD), key_rows, value_rows, counts_home)
        return result.reshape(REQ_DEV * REQ_LEN, query_cols)
    stacked = lax.map(one_home, (tokens.reshape(homes, REQ_DEV, REQ_LEN, D), request_adapter.reshape(homes, REQ_DEV), request_tokens.reshape(homes, REQ_DEV)))
    return stacked.reshape(TOKENS, query_cols)
```

```python
import functools
import math

import jax
import jax.numpy as jnp
import numpy as np
from jax import lax
from jax.experimental import pallas as pl
from jax.experimental.pallas import tpu as pltpu
from jax.sharding import Mesh
from jax.sharding import PartitionSpec as P

HD = 128
REQ_LEN = 14
SLOT = 16
PLANE = 4

rope_theta = 500000.0
BF16 = jnp.bfloat16
F32 = jnp.float32


def rope_tables(length, head_size):
    half_size = head_size // 2
    exponent = jnp.arange(half_size, dtype=jnp.float32) * (2.0 / head_size)
    frequency = rope_theta ** (-exponent)
    angles = jnp.arange(length, dtype=jnp.float32)[:, None] * frequency[None, :]
    angles = jnp.concatenate([angles, angles], axis=1)
    return (jnp.cos(angles), jnp.sin(angles))


def rotate(values, cosine, sine_table):
    half_size = values.shape[-1] // 2
    turned = jnp.concatenate([-values[..., half_size:], values[..., :half_size]], axis=-1)
    return values * cosine[:, None, :] + turned * sine_table[:, None, :]


def attend(queries, key_rows, value_rows, counts):
    length = queries.shape[1]
    scores = jnp.einsum("rikgd,rjkd->rkgij", queries, key_rows, preferred_element_type=jnp.float32)
    scores = scores * (1.0 / math.sqrt(queries.shape[-1]))
    position = jnp.arange(length, dtype=jnp.int32)
    causal = position[None, :] <= position[:, None]
    allowed = causal[None, :, :] & (position[None, None, :] < counts[:, None, None])
    scores = jnp.where(allowed[:, None, None, :, :], scores, -1e30)
    row_max = jnp.max(scores, axis=-1, keepdims=True)
    numerators = jnp.exp(scores - row_max)
    probabilities = (numerators / jnp.sum(numerators, axis=-1, keepdims=True)).astype(jnp.bfloat16)
    mixture = jnp.einsum(
        "rkgij,rjkd->rikgd", probabilities, value_rows, preferred_element_type=jnp.float32
    )
    live_rows = position[None, :] < counts[:, None]
    mixture = jnp.where(live_rows[:, :, None, None, None], mixture, 0.0)
    return mixture.astype(jnp.bfloat16)


def gather_body(
    tokens,
    w_query,
    w_keyvalue,
    adapter_down,
    adapter_up_query,
    adapter_up_value,
    request_adapter,
    request_tokens,
    adapter_owner,
):
    wide_count = lax.axis_size("wide")
    narrow_count = lax.axis_size("narrow")
    narrow_index = lax.axis_index("narrow")
    tok_rows = tokens.shape[0]
    width_model = tokens.shape[1]
    requests_here = tok_rows // REQ_LEN
    capacity = 2 * requests_here
    slice_width = width_model // narrow_count
    query_cols = w_query.shape[1]
    key_cols = w_keyvalue.shape[2]
    local_rank = adapter_down.shape[3]
    row_total = capacity * REQ_LEN
    table_index = jnp.arange(adapter_owner.shape[0], dtype=jnp.int32)
    matches = request_adapter[:, None] == table_index[None, :]
    my_groups = jnp.sum(jnp.where(matches, adapter_owner[None, :], 0), axis=1)
    dest_select = (my_groups[None, :] == jnp.arange(wide_count, dtype=jnp.int32)[:, None]).astype(
        jnp.bfloat16
    )
    own_slice = lax.dynamic_slice_in_dim(tokens, narrow_index * slice_width, slice_width, 1)
    own_slice = own_slice.reshape(requests_here, REQ_LEN, slice_width)
    outgoing = jnp.einsum(
        "dr,rlf->dlf", dest_select, own_slice, preferred_element_type=jnp.float32
    ).astype(jnp.bfloat16)
    out_flags = jnp.sum(dest_select.astype(jnp.float32), axis=1, keepdims=True).astype(jnp.bfloat16)
    arrived, arrived_flags = (
        lax.all_to_all(outgoing, "wide", split_axis=0, concat_axis=0, tiled=True),
        lax.all_to_all(out_flags, "wide", split_axis=0, concat_axis=0, tiled=True),
    )
    query_piece = lax.all_gather(w_query, "wide", axis=0, tiled=True)
    keyvalue_piece = lax.all_gather(w_keyvalue, "wide", axis=0, tiled=True)
    query_base = jnp.dot(tokens, query_piece, preferred_element_type=jnp.float32)
    flat_piece = keyvalue_piece.reshape(keyvalue_piece.shape[0], 2 * key_cols)
    keyvalue_sum = jnp.dot(tokens, flat_piece, preferred_element_type=jnp.float32)
    incoming = (arrived_flags[:, 0] > 0.5).astype(jnp.int32)
    arrival_rank = jnp.cumsum(incoming) - 1
    slot_index = jnp.arange(capacity, dtype=jnp.int32)[:, None]
    compact_select = ((incoming[None, :] == 1) & (arrival_rank[None, :] == slot_index)).astype(
        jnp.bfloat16
    )
    compacted = jnp.einsum(
        "kh,hlf->klf", compact_select, arrived, preferred_element_type=jnp.float32
    ).astype(jnp.bfloat16)
    held_rows = compacted.reshape(row_total, slice_width)
    down_local = adapter_down[0].reshape(width_model, 2 * local_rank)
    shrunk = jnp.dot(
        lax.all_gather(held_rows, "narrow", axis=1, tiled=True),
        down_local,
        preferred_element_type=jnp.float32,
    )
    shrunk = shrunk.reshape(row_total, 2, local_rank).astype(jnp.bfloat16)
    rank_piece = lax.all_gather(shrunk, "narrow", axis=2, tiled=True)
    query_sum = jnp.dot(
        rank_piece[:, 0, :], adapter_up_query[0], preferred_element_type=jnp.float32
    )
    value_sum = jnp.dot(
        rank_piece[:, 1, :], adapter_up_value[0], preferred_element_type=jnp.float32
    )
    deltas = jnp.concatenate([query_sum, value_sum], axis=1).astype(jnp.bfloat16)
    deltas = deltas.reshape(capacity, REQ_LEN, query_cols + key_cols)
    going_back = jnp.einsum(
        "kh,klc->hlc", compact_select, deltas, preferred_element_type=jnp.float32
    ).astype(jnp.bfloat16)
    returned = lax.all_to_all(going_back, "wide", split_axis=0, concat_axis=0, tiled=True)
    own_deltas = jnp.einsum(
        "dr,dlc->rlc", dest_select, returned, preferred_element_type=jnp.float32
    )
    cosine, sine_table = rope_tables(REQ_LEN, HD)
    local_heads = query_cols // HD
    local_kv = key_cols // HD
    queries = query_base.reshape(requests_here, REQ_LEN, query_cols) + own_deltas[:, :, :query_cols]
    queries = rotate(
        queries.reshape(requests_here, REQ_LEN, local_heads, HD), cosine, sine_table
    ).astype(jnp.bfloat16)
    key_rows = rotate(
        keyvalue_sum[:, :key_cols].reshape(requests_here, REQ_LEN, local_kv, HD), cosine, sine_table
    ).astype(jnp.bfloat16)
    value_rows = (
        keyvalue_sum[:, key_cols:].reshape(requests_here, REQ_LEN, key_cols)
        + own_deltas[:, :, query_cols:]
    )
    value_rows = value_rows.reshape(requests_here, REQ_LEN, local_kv, HD).astype(jnp.bfloat16)
    grouped = queries.reshape(requests_here, REQ_LEN, local_kv, local_heads // local_kv, HD)
    result = attend(grouped, key_rows, value_rows, request_tokens)
    return result.reshape(tok_rows, query_cols)


VMEM = pl.BlockSpec(memory_space=pltpu.VMEM)
SMEM = pl.BlockSpec(memory_space=pltpu.SMEM)
PARAMS = pltpu.CompilerParams(vmem_limit_bytes=16 * 2**20)

ORDER = ((3, 2, 1, 0), (3, 2, 0, 1), (0, 1, 3, 2), (0, 1, 2, 3))
SEND2 = (1, 0, 0, 1)
INWARD, MIDDLE, PAIRS = ((0, 1), (3, 2)), ((1, 2), (2, 1)), ((0, 1), (1, 0), (2, 3), (3, 2))


def call(kernel, out_shape, ins, flops=0, nbytes=0, scratch=(), name=None):
    arrays = [a for a, _ in ins]
    specs = [s for _, s in ins]
    many = isinstance(out_shape, (list, tuple))
    return pl.pallas_call(
        kernel,
        out_shape=out_shape,
        in_specs=specs,
        out_specs=[VMEM] * len(out_shape) if many else VMEM,
        scratch_shapes=list(scratch),
        compiler_params=PARAMS,
        cost_estimate=pl.CostEstimate(flops=flops, bytes_accessed=nbytes, transcendentals=0),
        name=name,
    )(*arrays)


def iota(shape, axis):
    return lax.broadcasted_iota(jnp.int32, shape, axis)


def over_len(index):
    return (index * 4682) >> 16


def dot(a, b, contract=((1,), (0,))):
    return lax.dot_general(a, b, (contract, ((), ())), preferred_element_type=F32)


def dispatch_kernel(requests_here, pos, tokens, slots, filled, sems):
    count, _, half = filled.shape
    columns = pl.ds(pl.multiple_of(pos[2] * half, half), half)
    filled[...] = jnp.zeros(filled.shape, filled.dtype)
    for r in range(requests_here):
        owner = pos[3 + requests_here + pos[3 + r]]
        filled[owner, 0:REQ_LEN, :] = tokens[r * REQ_LEN : (r + 1) * REQ_LEN, columns]
        mark = (iota((SLOT - REQ_LEN, 128), 0) == 0) & (iota((SLOT - REQ_LEN, 128), 1) == r)
        filled[owner, REQ_LEN:SLOT, 0:128] = mark.astype(F32).astype(BF16)
    copies = [
        pltpu.make_async_copy(filled.at[n], slots.at[n], sems.at[n]) for n in range(count)
    ]
    for copy in copies:
        copy.start()
    for copy in copies:
        copy.wait()


def slices_kernel(pos, tokens, *slices):
    z, q = pos[0], pos[1]
    count = len(slices)
    depth = slices[0].shape[1] // PLANE
    for shift, out in enumerate(slices):
        to = (z + shift) & (count - 1)
        for i in range(PLANE):
            start = pl.multiple_of((to * PLANE + (q ^ i)) * depth, depth)
            out[:, i * depth : (i + 1) * depth] = tokens[:, pl.ds(start, depth)]


def compact_kernel(pos, order, arrived, packed, select, marks):
    z, q = pos[0], pos[1]
    count = arrived.shape[0]
    rows = count * SLOT
    blocks = []
    for o in range(count):
        home = order[z, o // PLANE] * PLANE + (q ^ (o % PLANE))
        blocks.append(arrived[home])
    held = jnp.concatenate(blocks, axis=0)
    here = (iota((rows, 128), 0) & (SLOT - 1)) == REQ_LEN
    marked = jnp.where(here, held[:, :128].astype(F32), 0.0)
    marked = jnp.where(iota((rows, 128), 1) < 8, marked, 0.0).astype(BF16)
    marks[...] = marked
    row, col = iota((rows, rows), 0), iota((rows, rows), 1)
    same = ((row >> 4) == (col >> 4)).astype(F32).astype(BF16)
    which = dot(marked, same, ((0,), (0,)))
    present = jnp.sum(which, axis=0, keepdims=True)
    earlier = (((row & (SLOT - 1)) == 0) & ((row >> 4) < (col >> 4))).astype(F32).astype(BF16)
    rank = dot(jnp.broadcast_to(present, (8, rows)).astype(BF16), earlier)[:1]
    out_rows = packed.shape[0]
    k = over_len(iota((out_rows, rows), 0))
    place = iota((out_rows, rows), 0) - k * REQ_LEN
    chosen = (k.astype(F32) == rank) & (present > 0.5)
    chosen = chosen & (place == (iota((out_rows, rows), 1) & (SLOT - 1)))
    chosen = chosen.astype(F32).astype(BF16)
    select[...] = chosen
    packed[...] = dot(chosen, held).astype(BF16)


def shrink_kernel(pos, own, down, total):
    half = own.shape[1]
    mine = pl.ds(pl.multiple_of(pos[2] * half, half), half)
    total[...] = dot(own[...], down[mine, :])


def shrink_rest_kernel(pos, total, other, down, out):
    half = other.shape[1]
    theirs = pl.ds(pl.multiple_of((1 - pos[2]) * half, half), half)
    rows = total.shape[0]
    out[rows:, :] = jnp.zeros((out.shape[0] - rows, out.shape[1]), BF16)
    out[0:rows, :] = (total[...] + dot(other[...], down[theirs, :])).astype(BF16)


def expand_kernel(pos, own, other, select, marks, up_query, up_value, *outs):
    y = pos[2]
    rank = own.shape[1] // 2
    mine = pl.ds(pl.multiple_of(y * rank, rank), rank)
    theirs = pl.ds(pl.multiple_of((1 - y) * rank, rank), rank)
    chosen = select[...]
    rows = chosen.shape[0]
    own_rows = dot(chosen, own[0:rows, :], ((0,), (0,))).astype(BF16)
    other_rows = dot(chosen, other[0:rows, :], ((0,), (0,))).astype(BF16)
    query_cols = up_query.shape[1]
    for name, up, first in ((0, up_query, 0), (1, up_value, query_cols)):
        span = slice(name * rank, (name + 1) * rank)
        delta = dot(own_rows[:, span], up[mine, :]) + dot(other_rows[:, span], up[theirs, :])
        if name == 0:
            head = delta[:, :128] + marks[...].astype(F32)
            delta = jnp.concatenate([head, delta[:, 128:]], axis=1)
        delta = delta.astype(BF16)
        for i in range(PLANE):
            for b in range(4):
                start = (b * PLANE + i) * SLOT
                piece = delta[start : start + SLOT]
                out = outs[min(b, 2) * PLANE + i]
                at = max(b - 2, 0) * SLOT
                out[at : at + SLOT, first : first + up.shape[1]] = piece


def partial_kernel(pos, inverse, s0, s1, s2, s3, q0, q1, q2, q3, v0, v1, v2, v3, out_a, out_b, rows):
    z = pos[0]
    count, height, _ = out_a.shape
    padded = rows.shape[0] // count
    rows[...] = jnp.zeros(rows.shape, rows.dtype)
    for shift, s in enumerate((s0, s1, s2, s3)):
        rows[shift * padded : shift * padded + height, :] = s[...]
    tile = 512
    queries, values = (q0, q1, q2, q3), (v0, v1, v2, v3)
    spans = [(queries, n * tile) for n in range(q0.shape[1] // tile)]
    half = v0.shape[1] // 2
    spans += [(values, half + n * tile) for n in range(half // tile)]
    spans += [(values, n * tile) for n in range(half // tile)]
    for n, (refs, start) in enumerate(spans):
        weights = jnp.concatenate([r[:, start : start + tile] for r in refs], axis=0)
        total = dot(rows[...], weights)
        at = n * tile
        out, at = (out_a, at) if at < out_a.shape[2] else (out_b, at - out_a.shape[2])
        for shift in range(count):
            block = total[shift * padded : shift * padded + height]
            out[inverse[z, shift], :, at : at + tile] = block


def placed(height, pieces):
    held = jnp.concatenate(pieces, axis=0)
    rows = held.shape[0]
    here = (iota((rows, 128), 0) & (SLOT - 1)) == REQ_LEN
    marked = jnp.where(here, held[:, :128].astype(F32), 0.0).astype(BF16)
    same = ((iota((rows, rows), 0) >> 4) == (iota((rows, rows), 1) >> 4)).astype(F32).astype(BF16)
    which = dot(marked, same, ((0,), (0,))).astype(BF16)
    request = over_len(iota((height, 128), 0))
    chosen = dot((request == iota((height, 128), 1)).astype(F32).astype(BF16), which)
    t = iota((height, rows), 0)
    place = t - over_len(t) * REQ_LEN
    chosen = jnp.where(place == (iota((height, rows), 1) & (SLOT - 1)), chosen, 0.0).astype(BF16)
    return dot(chosen, held)


def add_into(out, base, terms, received):
    width = terms.shape[1]
    left = base[:, :width] + terms
    for r in received:
        left = left + r[:, :width].astype(F32)
    out[:, :width] = left.astype(out.dtype)
    if width < base.shape[1]:
        right = base[:, width:]
        for r in received:
            right = right + r[:, width:].astype(F32)
        out[:, width:] = right.astype(out.dtype)


def fill(base, entry, pieces, out_a, out_b):
    terms = placed(out_a.shape[0], pieces)
    cut = out_a.shape[1]
    add_into(out_a, base[0][entry], terms[:, :cut], [])
    add_into(out_b, base[1][entry], terms[:, cut:], [])


def first_kernel(base_a, base_b, d0, d1, d2, d3, out_a, out_b):
    fill((base_a, base_b), 0, [d[...] for d in (d0, d1, d2, d3)], out_a, out_b)


def next_kernel(base_a, base_b, d0, d1, d2, d3, out_a, out_b):
    fill((base_a, base_b), 1, [d[...] for d in (d0, d1, d2, d3)], out_a, out_b)


def rest_kernel(base_a, base_b, d0, d1, d2, d3, third_a, third_b, own_a, own_b):
    pieces = [d[...] for d in (d0, d1, d2, d3)]
    fill((base_a, base_b), 2, [d[0:SLOT] for d in pieces], third_a, third_b)
    fill((base_a, base_b), 3, [d[SLOT:] for d in pieces], own_a, own_b)


def second_kernel(pos, table, first, next_, received, out):
    own = jnp.where(table[0, pos[0]] == 0, first[...].astype(F32), next_[...])
    out[...] = (own + received[...].astype(F32)).astype(BF16)


def third_kernel(next_, third, from_end, from_middle, inner, outer):
    for own, received, out in ((next_, from_end, inner), (third, from_middle, outer)):
        out[...] = (own[...] + received[...].astype(F32)).astype(BF16)


def rotated(values, cosine, sine):
    return (values * cosine + pltpu.roll(values, HD // 2, 1) * sine).astype(BF16)


def attended(queries, keys, values, allowed, live):
    scale = 1.0 / math.sqrt(HD)
    scores = [
        jnp.where(allowed, dot(q, k, ((1,), (1,))) * scale, -1e30) for q, k in zip(queries, keys)
    ]
    weights = []
    for v in scores:
        v = jnp.exp(v - jnp.max(v, axis=1, keepdims=True))
        weights.append((v / jnp.sum(v, axis=1, keepdims=True)).astype(BF16))
    return [jnp.where(live, dot(w, v), 0.0).astype(BF16) for w, v in zip(weights, values)]


def attend_near_kernel(
    counts, own, up, down, cosine, sine, out, keys, values, allowed, live, total, queries
):
    height, near_cols = out.shape
    kv_heads = keys.shape[0]
    kv_cols = kv_heads * HD
    padded = allowed.shape[0] // (near_cols // HD)
    total[...] = own[...] + (up[...].astype(F32) + down[...].astype(F32))
    cos, sin = cosine[...], sine[...]
    queries[...] = jnp.zeros(queries.shape, BF16)
    keys[...] = jnp.zeros(keys.shape, BF16)
    values[...] = jnp.zeros(values.shape, BF16)
    for k in range(kv_heads):
        first = near_cols + k * HD
        values[k, 0:height, :] = total[:, first : first + HD].astype(BF16)
        first += kv_cols
        keys[k, 0:height, :] = rotated(total[:, first : first + HD], cos, sin)
    for g in range(near_cols // HD):
        head = total[:, g * HD : (g + 1) * HD]
        queries[g * padded : g * padded + height, :] = rotated(head, cos, sin)
    t, s = iota((padded, HD), 0), iota((padded, HD), 1)
    request_t, request_s = over_len(t), over_len(s)
    limit = jnp.zeros((padded, HD), jnp.int32)
    row_limit = jnp.zeros((padded, HD), jnp.int32)
    for r in range(counts.shape[0]):
        limit = jnp.where(request_s == r, counts[r], limit)
        row_limit = jnp.where(request_t == r, counts[r], row_limit)
    here = (request_t == request_s) & (s <= t) & (s - request_s * REQ_LEN < limit)
    alive = (t - request_t * REQ_LEN) < row_limit
    for mask, part in ((allowed, here), (live, alive)):
        mask[...] = jnp.concatenate([part.astype(F32)] * (near_cols // HD), axis=0)
    (mixed,) = attended(
        [queries[...]], [keys[kv_heads - 1]], [values[kv_heads - 1]], allowed[...] > 0.5, live[...] > 0.5
    )
    for g in range(near_cols // HD):
        out[:, g * HD : (g + 1) * HD] = mixed[g * padded : g * padded + height]


def attend_kernel(
    own, up, down, near, keys, values, allowed, live, cosine, sine, out, total, queries
):
    height, far_cols = own.shape
    kv_heads = queries.shape[0]
    group = far_cols // HD // kv_heads
    padded = queries.shape[1] // group
    total[...] = own[...] + (up[...].astype(F32) + down[...].astype(F32))
    cos, sin = cosine[...], sine[...]
    out[:, far_cols:] = near[...]
    queries[...] = jnp.zeros(queries.shape, BF16)
    for k in range(kv_heads):
        for g in range(group):
            h = k * group + g
            head = total[:, h * HD : (h + 1) * HD]
            queries[k, g * padded : g * padded + height, :] = rotated(head, cos, sin)
    heads = range(kv_heads)
    mixed = attended(
        [queries[k] for k in heads],
        [keys[k] for k in heads],
        [values[k] for k in heads],
        allowed[...] > 0.5,
        live[...] > 0.5,
    )
    for k in heads:
        for g in range(group):
            h = k * group + g
            out[:, h * HD : (h + 1) * HD] = mixed[k][g * padded : g * padded + height]


def reduce_body(
    tokens,
    w_query,
    w_keyvalue,
    adapter_down,
    adapter_up_query,
    adapter_up_value,
    request_adapter,
    request_tokens,
    adapter_owner,
):
    nz = lax.axis_size("z")
    z, q, y = lax.axis_index("z"), lax.axis_index("plane"), lax.axis_index("narrow")
    pos = jnp.stack([z, q, y]).astype(jnp.int32)
    order = np.array(ORDER, np.int32)
    inverse = np.zeros((nz, nz), np.int32)
    for at in range(nz):
        for shift in range(nz):
            inverse[at, shift] = ORDER[at].index((at - shift) % nz)
    order, inverse = jnp.asarray(order), jnp.asarray(inverse)
    table = jnp.asarray(np.array([SEND2], np.int32))
    height, width = tokens.shape
    homes = nz * PLANE
    requests_here = height // REQ_LEN
    capacity = 2 * requests_here
    half = width // 2
    query_cols, key_cols = w_query.shape[1], w_keyvalue.shape[2]
    delta_cols = query_cols + key_cols
    cols = query_cols + 2 * key_cols
    chunk_cols = cols // 2
    local_rank = adapter_down.shape[3]
    shape = jax.ShapeDtypeStruct
    barrier = lax.optimization_barrier
    by_c = [(0, 1), (1, 0), (2, 3), (3, 2)]
    by_x = [(0, 2), (2, 0), (1, 3), (3, 1)]
    by_xc = [(0, 3), (3, 0), (1, 2), (2, 1)]
    by_y = [(0, 1), (1, 0)]

    def plane(a, perm):
        return lax.ppermute(a, "plane", perm)

    pos = jnp.concatenate([pos, request_adapter, adapter_owner])
    in_hbm = pl.BlockSpec(memory_space=pltpu.HBM)
    slots = pl.pallas_call(
        functools.partial(dispatch_kernel, requests_here),
        out_shape=shape((homes, SLOT, half), BF16),
        in_specs=[SMEM, VMEM],
        out_specs=in_hbm,
        scratch_shapes=[
            pltpu.VMEM((homes, SLOT, half), BF16),
            pltpu.SemaphoreType.DMA((homes,)),
        ],
        compiler_params=PARAMS,
        name="dispatch",
    )(pos, tokens)
    arrived = lax.all_to_all(slots, ("z", "plane"), 0, 0, tiled=True)
    q_x = plane(w_query, by_x)
    w_keyvalue, w_query, _ = barrier((w_keyvalue, w_query, slots))
    w_kv = w_keyvalue.reshape(w_keyvalue.shape[0], 2 * key_cols)
    kv_x = plane(w_kv, by_x)
    down = adapter_down[0].reshape(width, 2 * local_rank)

    packed_rows = capacity * REQ_LEN
    packed, select, marks = call(
        compact_kernel,
        [
            shape((packed_rows, half), BF16),
            shape((packed_rows, homes * SLOT), BF16),
            shape((homes * SLOT, 128), BF16),
        ],
        [(pos, SMEM), (order, SMEM), (arrived, VMEM)],
        name="compact",
    )

    def rotate_z(a, shift):
        return lax.ppermute(a, "z", [(i, (i + shift) % nz) for i in range(nz)])

    packed_other = lax.ppermute(packed, "narrow", by_y)
    tokens, _ = barrier((tokens, packed))
    slices = call(
        slices_kernel,
        [shape((height, width // nz), BF16)] * nz,
        [(pos, SMEM), (tokens, VMEM)],
        name="slices",
    )
    s1, s2 = rotate_z(slices[1], 1), rotate_z(slices[2], 2)
    total = call(
        shrink_kernel,
        shape((packed_rows, 2 * local_rank), F32),
        [(pos, SMEM), (packed, VMEM), (down, VMEM)],
        name="shrink",
    )
    packed_other, s1, s2, total, q_x = barrier((packed_other, s1, s2, total, q_x))
    q_xc = plane(q_x, by_c)
    shrunk = call(
        shrink_rest_kernel,
        shape((packed_rows + SLOT, 2 * local_rank), BF16),
        [(pos, SMEM), (total, VMEM), (packed_other, VMEM), (down, VMEM)],
        name="shrink_rest",
    )
    shrunk_other = lax.ppermute(shrunk, "narrow", by_y)
    slices, w_query, w_kv, _ = barrier((slices, w_query, w_kv, shrunk))
    q_c, kv_c = plane(w_query, by_c), plane(w_kv, by_c)
    s3 = rotate_z(slices[3], 3)
    shrunk_other, kv_x = barrier((shrunk_other, kv_x))
    slices = [slices[0], s1, s2]
    pieces = call(
        expand_kernel,
        [shape((SLOT, delta_cols), BF16)] * (2 * PLANE)
        + [shape((2 * SLOT, delta_cols), BF16)] * PLANE,
        [
            (pos, SMEM),
            (shrunk, VMEM),
            (shrunk_other, VMEM),
            (select, VMEM),
            (marks, VMEM),
            (adapter_up_query[0], VMEM),
            (adapter_up_value[0], VMEM),
        ],
        name="expand",
    )

    def over_plane(four):
        return [four[0]] + [
            plane(four[i], perm) for i, perm in ((1, by_c), (2, by_x), (3, by_xc))
        ]

    first = over_plane(pieces[:PLANE])
    slices, kv_x, s3, _ = barrier((slices, kv_x, s3, pieces))
    slices = slices + [s3]
    kv_xc = plane(kv_x, by_c)
    padded = -(-height // SLOT) * SLOT
    base_a, base_b = call(
        partial_kernel,
        [shape((nz, height, chunk_cols), F32)] * 2,
        [(pos, SMEM), (inverse, SMEM)]
        + [(s, VMEM) for s in slices]
        + [(w, VMEM) for w in (w_query, q_c, q_x, q_xc, w_kv, kv_c, kv_x, kv_xc)],
        flops=2 * nz * height * width // nz * cols,
        nbytes=16 * 2**20,
        scratch=[pltpu.VMEM((nz * (-(-height // 8) * 8), width // nz), BF16)],
        name="partial",
    )
    block = shape((height, chunk_cols), BF16)
    wide_block = shape((height, chunk_cols), F32)
    bases = [(base_a, VMEM), (base_b, VMEM)]

    def of(four):
        return [(p, VMEM) for p in four]

    sent = call(first_kernel, [block, block], bases + of(first), name="reduce_first")
    received = [lax.ppermute(s, "z", INWARD) for s in sent]
    pieces, _ = barrier((pieces, sent))
    next_ = over_plane(pieces[PLANE : 2 * PLANE])
    rest = over_plane(pieces[2 * PLANE :])
    second = call(next_kernel, [wide_block] * 2, bases + of(next_), name="reduce_next")
    received[0], rest = barrier((received[0], rest))
    *third, own_a, own_b = call(rest_kernel, [wide_block] * 4, bases + of(rest), name="reduce_rest")
    scalars = [(pos, SMEM), (table, SMEM)]
    ends, middles = [], []
    for chunk in range(2):
        out = call(
            second_kernel,
            block,
            scalars + of([sent[chunk], second[chunk], received[chunk]]),
            name="reduce_second",
        )
        middles.append(lax.ppermute(out, "z", MIDDLE))
        ends.append(lax.ppermute(out, "z", INWARD))
    for chunk in range(2):
        inner, outer = call(
            third_kernel,
            [block, block],
            of([second[chunk], third[chunk], ends[chunk], middles[chunk]]),
            name="reduce_third",
        )
        middles[chunk] = lax.ppermute(inner, "z", MIDDLE)
        ends[chunk] = lax.ppermute(outer, "z", PAIRS)

    angles = np.arange(REQ_LEN)[:, None] * (rope_theta ** (-np.arange(HD // 2) * (2.0 / HD)))[None, :]
    cosine = np.tile(np.concatenate([np.cos(angles)] * 2, axis=1), (requests_here, 1))
    sine = np.tile(np.concatenate([-np.sin(angles), np.sin(angles)], axis=1), (requests_here, 1))
    tables = [(jnp.asarray(a.astype(np.float32)), VMEM) for a in (cosine, sine)]
    near_cols = query_cols - chunk_cols
    group_rows = query_cols // key_cols * padded
    key_heads = key_cols // HD
    held = shape((key_heads, HD, HD), BF16)
    mask = shape((group_rows, HD), F32)
    near = call(
        attend_near_kernel,
        [shape((height, near_cols), BF16), held, held, mask, mask],
        [(request_tokens, SMEM)] + of([own_b, ends[1], middles[1]]) + tables,
        nbytes=8 * 2**20,
        scratch=[pltpu.VMEM((height, chunk_cols), F32), pltpu.VMEM((group_rows, HD), BF16)],
        name="attend_near",
    )
    return call(
        attend_kernel,
        shape((height, query_cols), BF16),
        of([own_a, ends[0], middles[0], *near]) + tables,
        scratch=[
            pltpu.VMEM((height, chunk_cols), F32),
            pltpu.VMEM((key_heads - 1, group_rows, HD), BF16),
        ],
        name="attend",
    )


def solution(mesh):
    wide, narrow = mesh.shape["wide"], mesh.shape["narrow"]
    if wide == 4 * PLANE and narrow == 2:
        grid = Mesh(mesh.devices.reshape(wide // PLANE, PLANE, narrow), ("z", "plane", "narrow"))
        body, on, over = reduce_body, grid, ("z", "plane")
    else:
        body, on, over = gather_body, mesh, "wide"
    return jax.shard_map(
        body,
        mesh=on,
        in_specs=(
            P(over, None),
            P(over, "narrow"),
            P(over, None, "narrow"),
            P(over, None, None, "narrow"),
            P(over, None, "narrow"),
            P(over, None, "narrow"),
            P(over),
            P(over),
            P(),
        ),
        out_specs=P(over, "narrow"),
        check_vma=False,
    )
```

```python
import functools
import math

import jax
import jax.numpy as jnp
import numpy as np
from jax import lax
from jax.experimental import pallas as pl
from jax.experimental.pallas import tpu as pltpu
from jax.sharding import Mesh
from jax.sharding import PartitionSpec as P

HD = 128
REQ_LEN = 14
SLOT = 16
PLANE = 4

rope_theta = 500000.0
BF16 = jnp.bfloat16
F32 = jnp.float32


def rope_tables(length, head_size):
    half_size = head_size // 2
    exponent = jnp.arange(half_size, dtype=jnp.float32) * (2.0 / head_size)
    frequency = rope_theta ** (-exponent)
    angles = jnp.arange(length, dtype=jnp.float32)[:, None] * frequency[None, :]
    angles = jnp.concatenate([angles, angles], axis=1)
    return (jnp.cos(angles), jnp.sin(angles))


def rotate(values, cosine, sine_table):
    half_size = values.shape[-1] // 2
    turned = jnp.concatenate([-values[..., half_size:], values[..., :half_size]], axis=-1)
    return values * cosine[:, None, :] + turned * sine_table[:, None, :]


def attend(queries, key_rows, value_rows, counts):
    length = queries.shape[1]
    scores = jnp.einsum("rikgd,rjkd->rkgij", queries, key_rows, preferred_element_type=jnp.float32)
    scores = scores * (1.0 / math.sqrt(queries.shape[-1]))
    position = jnp.arange(length, dtype=jnp.int32)
    causal = position[None, :] <= position[:, None]
    allowed = causal[None, :, :] & (position[None, None, :] < counts[:, None, None])
    scores = jnp.where(allowed[:, None, None, :, :], scores, -1e30)
    row_max = jnp.max(scores, axis=-1, keepdims=True)
    numerators = jnp.exp(scores - row_max)
    probabilities = (numerators / jnp.sum(numerators, axis=-1, keepdims=True)).astype(jnp.bfloat16)
    mixture = jnp.einsum(
        "rkgij,rjkd->rikgd", probabilities, value_rows, preferred_element_type=jnp.float32
    )
    live_rows = position[None, :] < counts[:, None]
    mixture = jnp.where(live_rows[:, :, None, None, None], mixture, 0.0)
    return mixture.astype(jnp.bfloat16)


def gather_body(
    tokens,
    w_query,
    w_keyvalue,
    adapter_down,
    adapter_up_query,
    adapter_up_value,
    request_adapter,
    request_tokens,
    adapter_owner,
):
    wide_count = lax.axis_size("wide")
    narrow_count = lax.axis_size("narrow")
    narrow_index = lax.axis_index("narrow")
    tok_rows = tokens.shape[0]
    width_model = tokens.shape[1]
    requests_here = tok_rows // REQ_LEN
    capacity = 2 * requests_here
    slice_width = width_model // narrow_count
    query_cols = w_query.shape[1]
    key_cols = w_keyvalue.shape[2]
    local_rank = adapter_down.shape[3]
    row_total = capacity * REQ_LEN
    table_index = jnp.arange(adapter_owner.shape[0], dtype=jnp.int32)
    matches = request_adapter[:, None] == table_index[None, :]
    my_groups = jnp.sum(jnp.where(matches, adapter_owner[None, :], 0), axis=1)
    dest_select = (my_groups[None, :] == jnp.arange(wide_count, dtype=jnp.int32)[:, None]).astype(
        jnp.bfloat16
    )
    own_slice = lax.dynamic_slice_in_dim(tokens, narrow_index * slice_width, slice_width, 1)
    own_slice = own_slice.reshape(requests_here, REQ_LEN, slice_width)
    outgoing = jnp.einsum(
        "dr,rlf->dlf", dest_select, own_slice, preferred_element_type=jnp.float32
    ).astype(jnp.bfloat16)
    out_flags = jnp.sum(dest_select.astype(jnp.float32), axis=1, keepdims=True).astype(jnp.bfloat16)
    arrived, arrived_flags = (
        lax.all_to_all(outgoing, "wide", split_axis=0, concat_axis=0, tiled=True),
        lax.all_to_all(out_flags, "wide", split_axis=0, concat_axis=0, tiled=True),
    )
    query_piece = lax.all_gather(w_query, "wide", axis=0, tiled=True)
    keyvalue_piece = lax.all_gather(w_keyvalue, "wide", axis=0, tiled=True)
    query_base = jnp.dot(tokens, query_piece, preferred_element_type=jnp.float32)
    flat_piece = keyvalue_piece.reshape(keyvalue_piece.shape[0], 2 * key_cols)
    keyvalue_sum = jnp.dot(tokens, flat_piece, preferred_element_type=jnp.float32)
    incoming = (arrived_flags[:, 0] > 0.5).astype(jnp.int32)
    arrival_rank = jnp.cumsum(incoming) - 1
    slot_index = jnp.arange(capacity, dtype=jnp.int32)[:, None]
    compact_select = ((incoming[None, :] == 1) & (arrival_rank[None, :] == slot_index)).astype(
        jnp.bfloat16
    )
    compacted = jnp.einsum(
        "kh,hlf->klf", compact_select, arrived, preferred_element_type=jnp.float32
    ).astype(jnp.bfloat16)
    held_rows = compacted.reshape(row_total, slice_width)
    down_local = adapter_down[0].reshape(width_model, 2 * local_rank)
    shrunk = jnp.dot(
        lax.all_gather(held_rows, "narrow", axis=1, tiled=True),
        down_local,
        preferred_element_type=jnp.float32,
    )
    shrunk = shrunk.reshape(row_total, 2, local_rank).astype(jnp.bfloat16)
    rank_piece = lax.all_gather(shrunk, "narrow", axis=2, tiled=True)
    query_sum = jnp.dot(
        rank_piece[:, 0, :], adapter_up_query[0], preferred_element_type=jnp.float32
    )
    value_sum = jnp.dot(
        rank_piece[:, 1, :], adapter_up_value[0], preferred_element_type=jnp.float32
    )
    deltas = jnp.concatenate([query_sum, value_sum], axis=1).astype(jnp.bfloat16)
    deltas = deltas.reshape(capacity, REQ_LEN, query_cols + key_cols)
    going_back = jnp.einsum(
        "kh,klc->hlc", compact_select, deltas, preferred_element_type=jnp.float32
    ).astype(jnp.bfloat16)
    returned = lax.all_to_all(going_back, "wide", split_axis=0, concat_axis=0, tiled=True)
    own_deltas = jnp.einsum(
        "dr,dlc->rlc", dest_select, returned, preferred_element_type=jnp.float32
    )
    cosine, sine_table = rope_tables(REQ_LEN, HD)
    local_heads = query_cols // HD
    local_kv = key_cols // HD
    queries = query_base.reshape(requests_here, REQ_LEN, query_cols) + own_deltas[:, :, :query_cols]
    queries = rotate(
        queries.reshape(requests_here, REQ_LEN, local_heads, HD), cosine, sine_table
    ).astype(jnp.bfloat16)
    key_rows = rotate(
        keyvalue_sum[:, :key_cols].reshape(requests_here, REQ_LEN, local_kv, HD), cosine, sine_table
    ).astype(jnp.bfloat16)
    value_rows = (
        keyvalue_sum[:, key_cols:].reshape(requests_here, REQ_LEN, key_cols)
        + own_deltas[:, :, query_cols:]
    )
    value_rows = value_rows.reshape(requests_here, REQ_LEN, local_kv, HD).astype(jnp.bfloat16)
    grouped = queries.reshape(requests_here, REQ_LEN, local_kv, local_heads // local_kv, HD)
    result = attend(grouped, key_rows, value_rows, request_tokens)
    return result.reshape(tok_rows, query_cols)


VMEM = pl.BlockSpec(memory_space=pltpu.VMEM)
SMEM = pl.BlockSpec(memory_space=pltpu.SMEM)
PARAMS = pltpu.CompilerParams(vmem_limit_bytes=16 * 2**20)

ORDER = ((3, 2, 1, 0), (3, 2, 0, 1), (0, 1, 3, 2), (0, 1, 2, 3))
SEND2 = (1, 0, 0, 1)
INWARD, MIDDLE, PAIRS = ((0, 1), (3, 2)), ((1, 2), (2, 1)), ((0, 1), (1, 0), (2, 3), (3, 2))


def call(kernel, out_shape, ins, flops=0, nbytes=0, scratch=(), name=None):
    arrays = [a for a, _ in ins]
    specs = [s for _, s in ins]
    many = isinstance(out_shape, (list, tuple))
    return pl.pallas_call(
        kernel,
        out_shape=out_shape,
        in_specs=specs,
        out_specs=[VMEM] * len(out_shape) if many else VMEM,
        scratch_shapes=list(scratch),
        compiler_params=PARAMS,
        cost_estimate=pl.CostEstimate(flops=flops, bytes_accessed=nbytes, transcendentals=0),
        name=name,
    )(*arrays)


def iota(shape, axis):
    return lax.broadcasted_iota(jnp.int32, shape, axis)


def over_len(index):
    return (index * 4682) >> 16


def dot(a, b, contract=((1,), (0,))):
    return lax.dot_general(a, b, (contract, ((), ())), preferred_element_type=F32)


def owner_of(pos, requests_here, r):
    return pos[3 + requests_here + pos[3 + r]]


def dispatch_kernel(requests_here, pos, tokens, slots, filled, sems):
    count, _, main = filled.shape
    half = main * SLOT // REQ_LEN
    tail = half - main
    height = tokens.shape[0]
    first = pl.multiple_of(pos[2] * half, half)
    filled[...] = jnp.zeros(filled.shape, filled.dtype)
    tails = tokens[:, pl.ds(pl.multiple_of(first + main, 128), tail)]
    packed = 2 * requests_here
    target, source = iota((packed, height), 0), iota((packed, height), 1)
    parts = []
    for j in range(REQ_LEN // 2):
        pick = (source == target * (REQ_LEN // 2) + j).astype(F32).astype(BF16)
        parts.append(dot(pick, tails).astype(BF16))
    for r in range(requests_here):
        owner = owner_of(pos, requests_here, r)
        filled[owner, 0:REQ_LEN, :] = tokens[r * REQ_LEN : (r + 1) * REQ_LEN, pl.ds(first, main)]
        for j, part in enumerate(parts):
            filled[owner, REQ_LEN:SLOT, j * tail : (j + 1) * tail] = part[2 * r : 2 * r + 2]
    copies = [
        pltpu.make_async_copy(filled.at[n], slots.at[n], sems.at[n]) for n in range(count)
    ]
    for copy in copies:
        copy.start()
    for copy in copies:
        copy.wait()


def slices_kernel(requests_here, pos, tokens, *slices):
    z, q = pos[0], pos[1]
    count = len(slices)
    height = tokens.shape[0]
    depth = slices[0].shape[1] // PLANE
    spare = slices[0].shape[0] - height
    lane = iota((spare, 128), 1)
    owners = jnp.zeros((spare, 128), F32)
    for r in range(requests_here):
        owner = owner_of(pos, requests_here, r).astype(F32)
        owners = jnp.where(lane == r, owner, owners)
    for shift, out in enumerate(slices):
        to = (z + shift) & (count - 1)
        for i in range(PLANE):
            start = pl.multiple_of((to * PLANE + (q ^ i)) * depth, depth)
            out[0:height, i * depth : (i + 1) * depth] = tokens[:, pl.ds(start, depth)]
        out[height:, :] = jnp.zeros((spare, out.shape[1]), BF16)
        out[height:, 0:128] = owners.astype(BF16)


def compact_kernel(pos, order, arrived, packed, select):
    z, q = pos[0], pos[1]
    count, _, main = arrived.shape
    rows = count * SLOT
    blocks = []
    for o in range(count):
        home = order[z, o // PLANE] * PLANE + (q ^ (o % PLANE))
        blocks.append(arrived[home])
    held = jnp.concatenate(blocks, axis=0)
    top = jnp.zeros((rows, 128), F32)
    for c in range(main // 128):
        top = jnp.maximum(top, jnp.abs(held[:, c * 128 : (c + 1) * 128].astype(F32)))
    used = (top > 0.0).astype(F32).astype(BF16)
    row, col = iota((rows, rows), 0), iota((rows, rows), 1)
    same = ((row >> 4) == (col >> 4)).astype(F32).astype(BF16)
    present = jnp.sum(dot(used, same, ((0,), (0,))), axis=0, keepdims=True)
    present = (present > 0.5).astype(F32)
    earlier = (((row & (SLOT - 1)) == 0) & ((row >> 4) < (col >> 4))).astype(F32).astype(BF16)
    rank = dot(jnp.broadcast_to(present, (8, rows)).astype(BF16), earlier)[:1]
    out_rows = packed.shape[0]
    k = over_len(iota((out_rows, rows), 0))
    place = iota((out_rows, rows), 0) - k * REQ_LEN
    at = iota((out_rows, rows), 1) & (SLOT - 1)
    here = (k.astype(F32) == rank) & (present > 0.5)
    chosen = (here & (place == at)).astype(F32).astype(BF16)
    select[...] = chosen
    packed[:, :main] = dot(chosen, held).astype(BF16)
    tail = packed.shape[1] - main
    second = (place >= REQ_LEN // 2).astype(jnp.int32)
    turn = place - second * (REQ_LEN // 2)
    here = here & (at == REQ_LEN + second)
    total = jnp.zeros((out_rows, tail), F32)
    for j in range(REQ_LEN // 2):
        chosen = (here & (turn == j)).astype(F32).astype(BF16)
        total += dot(chosen, held[:, j * tail : (j + 1) * tail])
    packed[:, main:] = total.astype(BF16)


def shrink_kernel(pos, own, down, total):
    half = own.shape[1]
    mine = pl.ds(pl.multiple_of(pos[2] * half, half), half)
    total[...] = dot(own[...], down[mine, :])


def shrink_rest_kernel(pos, total, other, down, out):
    half = other.shape[1]
    theirs = pl.ds(pl.multiple_of((1 - pos[2]) * half, half), half)
    rows = total.shape[0]
    out[rows:, :] = jnp.zeros((out.shape[0] - rows, out.shape[1]), BF16)
    out[0:rows, :] = (total[...] + dot(other[...], down[theirs, :])).astype(BF16)


def expand_kernel(pos, own, other, select, up_query, up_value, *outs):
    y = pos[2]
    rank = own.shape[1] // 2
    mine = pl.ds(pl.multiple_of(y * rank, rank), rank)
    theirs = pl.ds(pl.multiple_of((1 - y) * rank, rank), rank)
    chosen = select[...]
    rows = chosen.shape[0]
    own_rows = dot(chosen, own[0:rows, :], ((0,), (0,))).astype(BF16)
    other_rows = dot(chosen, other[0:rows, :], ((0,), (0,))).astype(BF16)
    query_cols = up_query.shape[1]
    for name, up, first in ((0, up_query, 0), (1, up_value, query_cols)):
        span = slice(name * rank, (name + 1) * rank)
        delta = dot(own_rows[:, span], up[mine, :]) + dot(other_rows[:, span], up[theirs, :])
        delta = delta.astype(BF16)
        for i in range(PLANE):
            for b in range(4):
                start = (b * PLANE + i) * SLOT
                piece = delta[start : start + SLOT]
                out = outs[min(b, 2) * PLANE + i]
                at = max(b - 2, 0) * SLOT
                out[at : at + SLOT, first : first + up.shape[1]] = piece


def partial_kernel(pos, inverse, s0, s1, s2, s3, q0, q1, q2, q3, v0, v1, v2, v3, out_a, out_b, owners, rows):
    z = pos[0]
    count, height, _ = out_a.shape
    padded = rows.shape[0] // count
    owners[...] = jnp.zeros(owners.shape, owners.dtype)
    for shift, s in enumerate((s0, s1, s2, s3)):
        rows[shift * padded : (shift + 1) * padded, :] = s[...]
        owners[inverse[z, shift], 0 : padded - height, :] = s[height:, 0:128]
    tile = 512
    queries, values = (q0, q1, q2, q3), (v0, v1, v2, v3)
    spans = [(queries, n * tile) for n in range(q0.shape[1] // tile)]
    half = v0.shape[1] // 2
    spans += [(values, half + n * tile) for n in range(half // tile)]
    spans += [(values, n * tile) for n in range(half // tile)]
    for n, (refs, start) in enumerate(spans):
        weights = jnp.concatenate([r[:, start : start + tile] for r in refs], axis=0)
        total = dot(rows[...], weights)
        at = n * tile
        out, at = (out_a, at) if at < out_a.shape[2] else (out_b, at - out_a.shape[2])
        for shift in range(count):
            block = total[shift * padded : shift * padded + height]
            out[inverse[z, shift], :, at : at + tile] = block


def placed(height, pieces, owners, pos):
    held = jnp.concatenate(pieces, axis=0)
    rows = held.shape[0]
    request = over_len(iota((height, 128), 0))
    mine = (request == iota((height, 128), 1)).astype(F32).astype(BF16)
    owner = dot(mine, owners, ((1,), (1,)))[:, 0:1]
    t, slot = iota((height, rows), 0), iota((height, rows), 1)
    place = t - over_len(t) * REQ_LEN
    sender = (pos[0] * PLANE + (pos[1] ^ (slot >> 4))).astype(F32)
    chosen = (owner == sender) & (place == (slot & (SLOT - 1)))
    return dot(chosen.astype(F32).astype(BF16), held)


def add_into(out, base, terms, received):
    width = terms.shape[1]
    left = base[:, :width] + terms
    for r in received:
        left = left + r[:, :width].astype(F32)
    out[:, :width] = left.astype(out.dtype)
    if width < base.shape[1]:
        right = base[:, width:]
        for r in received:
            right = right + r[:, width:].astype(F32)
        out[:, width:] = right.astype(out.dtype)


def fill(pos, base, owners, entry, pieces, out_a, out_b):
    terms = placed(out_a.shape[0], pieces, owners[entry], pos)
    cut = out_a.shape[1]
    add_into(out_a, base[0][entry], terms[:, :cut], [])
    add_into(out_b, base[1][entry], terms[:, cut:], [])


def fill_kernel(entry, pos, base_a, base_b, owners, d0, d1, d2, d3, out_a, out_b):
    pieces = [d[...] for d in (d0, d1, d2, d3)]
    fill(pos, (base_a, base_b), owners, entry, pieces, out_a, out_b)


def rest_kernel(pos, base_a, base_b, owners, d0, d1, d2, d3, third_a, third_b, own_a, own_b):
    pieces = [d[...] for d in (d0, d1, d2, d3)]
    fill(pos, (base_a, base_b), owners, 2, [d[0:SLOT] for d in pieces], third_a, third_b)
    fill(pos, (base_a, base_b), owners, 3, [d[SLOT:] for d in pieces], own_a, own_b)


def second_kernel(pos, table, first, next_, received, out):
    own = jnp.where(table[0, pos[0]] == 0, first[...].astype(F32), next_[...])
    out[...] = (own + received[...].astype(F32)).astype(BF16)


def third_kernel(next_, third, from_end, from_middle, inner, outer):
    for own, received, out in ((next_, from_end, inner), (third, from_middle, outer)):
        out[...] = (own[...] + received[...].astype(F32)).astype(BF16)


def rotated(values, cosine, sine):
    return (values * cosine + pltpu.roll(values, HD // 2, 1) * sine).astype(BF16)


def attended(queries, keys, values, allowed, live):
    scale = 1.0 / math.sqrt(HD)
    scores = [
        jnp.where(allowed, dot(q, k, ((1,), (1,))) * scale, -1e30) for q, k in zip(queries, keys)
    ]
    weights = []
    for v in scores:
        v = jnp.exp(v - jnp.max(v, axis=1, keepdims=True))
        weights.append((v / jnp.sum(v, axis=1, keepdims=True)).astype(BF16))
    return [jnp.where(live, dot(w, v), 0.0).astype(BF16) for w, v in zip(weights, values)]


def attend_near_kernel(
    counts, own, up, down, cosine, sine, out, keys, values, allowed, live, total, queries
):
    height, near_cols = out.shape
    kv_heads = keys.shape[0]
    kv_cols = kv_heads * HD
    padded = allowed.shape[0] // (near_cols // HD)
    total[...] = own[...] + (up[...].astype(F32) + down[...].astype(F32))
    cos, sin = cosine[...], sine[...]
    queries[...] = jnp.zeros(queries.shape, BF16)
    keys[...] = jnp.zeros(keys.shape, BF16)
    values[...] = jnp.zeros(values.shape, BF16)
    for k in range(kv_heads):
        first = near_cols + k * HD
        values[k, 0:height, :] = total[:, first : first + HD].astype(BF16)
        first += kv_cols
        keys[k, 0:height, :] = rotated(total[:, first : first + HD], cos, sin)
    for g in range(near_cols // HD):
        head = total[:, g * HD : (g + 1) * HD]
        queries[g * padded : g * padded + height, :] = rotated(head, cos, sin)
    t, s = iota((padded, HD), 0), iota((padded, HD), 1)
    request_t, request_s = over_len(t), over_len(s)
    limit = jnp.zeros((padded, HD), jnp.int32)
    row_limit = jnp.zeros((padded, HD), jnp.int32)
    for r in range(counts.shape[0]):
        limit = jnp.where(request_s == r, counts[r], limit)
        row_limit = jnp.where(request_t == r, counts[r], row_limit)
    here = (request_t == request_s) & (s <= t) & (s - request_s * REQ_LEN < limit)
    alive = (t - request_t * REQ_LEN) < row_limit
    for mask, part in ((allowed, here), (live, alive)):
        mask[...] = jnp.concatenate([part.astype(F32)] * (near_cols // HD), axis=0)
    (mixed,) = attended(
        [queries[...]], [keys[kv_heads - 1]], [values[kv_heads - 1]], allowed[...] > 0.5, live[...] > 0.5
    )
    for g in range(near_cols // HD):
        out[:, g * HD : (g + 1) * HD] = mixed[g * padded : g * padded + height]


def attend_kernel(
    own, up, down, near, keys, values, allowed, live, cosine, sine, out, total, queries
):
    height, far_cols = own.shape
    kv_heads = queries.shape[0]
    group = far_cols // HD // kv_heads
    padded = queries.shape[1] // group
    total[...] = own[...] + (up[...].astype(F32) + down[...].astype(F32))
    cos, sin = cosine[...], sine[...]
    out[:, far_cols:] = near[...]
    queries[...] = jnp.zeros(queries.shape, BF16)
    for k in range(kv_heads):
        for g in range(group):
            h = k * group + g
            head = total[:, h * HD : (h + 1) * HD]
            queries[k, g * padded : g * padded + height, :] = rotated(head, cos, sin)
    heads = range(kv_heads)
    mixed = attended(
        [queries[k] for k in heads],
        [keys[k] for k in heads],
        [values[k] for k in heads],
        allowed[...] > 0.5,
        live[...] > 0.5,
    )
    for k in heads:
        for g in range(group):
            h = k * group + g
            out[:, h * HD : (h + 1) * HD] = mixed[k][g * padded : g * padded + height]


def reduce_body(
    tokens,
    w_query,
    w_keyvalue,
    adapter_down,
    adapter_up_query,
    adapter_up_value,
    request_adapter,
    request_tokens,
    adapter_owner,
):
    nz = lax.axis_size("z")
    z, q, y = lax.axis_index("z"), lax.axis_index("plane"), lax.axis_index("narrow")
    pos = jnp.stack([z, q, y]).astype(jnp.int32)
    order = np.array(ORDER, np.int32)
    inverse = np.zeros((nz, nz), np.int32)
    for at in range(nz):
        for shift in range(nz):
            inverse[at, shift] = ORDER[at].index((at - shift) % nz)
    order, inverse = jnp.asarray(order), jnp.asarray(inverse)
    table = jnp.asarray(np.array([SEND2], np.int32))
    height, width = tokens.shape
    homes = nz * PLANE
    requests_here = height // REQ_LEN
    capacity = 2 * requests_here
    half = width // 2
    main = half * REQ_LEN // SLOT
    sliced = -(-height // 8) * 8
    query_cols, key_cols = w_query.shape[1], w_keyvalue.shape[2]
    delta_cols = query_cols + key_cols
    cols = query_cols + 2 * key_cols
    chunk_cols = cols // 2
    local_rank = adapter_down.shape[3]
    shape = jax.ShapeDtypeStruct
    barrier = lax.optimization_barrier
    by_c = [(0, 1), (1, 0), (2, 3), (3, 2)]
    by_x = [(0, 2), (2, 0), (1, 3), (3, 1)]
    by_xc = [(0, 3), (3, 0), (1, 2), (2, 1)]
    by_y = [(0, 1), (1, 0)]

    def plane(a, perm):
        return lax.ppermute(a, "plane", perm)

    pos = jnp.concatenate([pos, request_adapter, adapter_owner])
    in_hbm = pl.BlockSpec(memory_space=pltpu.HBM)
    slots = pl.pallas_call(
        functools.partial(dispatch_kernel, requests_here),
        out_shape=shape((homes, SLOT, main), BF16),
        in_specs=[SMEM, VMEM],
        out_specs=in_hbm,
        scratch_shapes=[
            pltpu.VMEM((homes, SLOT, main), BF16),
            pltpu.SemaphoreType.DMA((homes,)),
        ],
        compiler_params=PARAMS,
        name="dispatch",
    )(pos, tokens)
    arrived = lax.all_to_all(slots, ("z", "plane"), 0, 0, tiled=True)
    q_x = plane(w_query, by_x)
    w_keyvalue, w_query, _ = barrier((w_keyvalue, w_query, slots))
    w_kv = w_keyvalue.reshape(w_keyvalue.shape[0], 2 * key_cols)
    kv_x = plane(w_kv, by_x)
    down = adapter_down[0].reshape(width, 2 * local_rank)

    packed_rows = capacity * REQ_LEN
    packed, select = call(
        compact_kernel,
        [
            shape((packed_rows, half), BF16),
            shape((packed_rows, homes * SLOT), BF16),
        ],
        [(pos, SMEM), (order, SMEM), (arrived, VMEM)],
        name="compact",
    )

    def rotate_z(a, shift):
        return lax.ppermute(a, "z", [(i, (i + shift) % nz) for i in range(nz)])

    packed_other = lax.ppermute(packed, "narrow", by_y)
    tokens, _ = barrier((tokens, packed))
    slices = call(
        functools.partial(slices_kernel, requests_here),
        [shape((sliced, width // nz), BF16)] * nz,
        [(pos, SMEM), (tokens, VMEM)],
        name="slices",
    )
    s1, s2 = rotate_z(slices[1], 1), rotate_z(slices[2], 2)
    total = call(
        shrink_kernel,
        shape((packed_rows, 2 * local_rank), F32),
        [(pos, SMEM), (packed, VMEM), (down, VMEM)],
        name="shrink",
    )
    packed_other, s1, s2, total, q_x = barrier((packed_other, s1, s2, total, q_x))
    q_xc = plane(q_x, by_c)
    shrunk = call(
        shrink_rest_kernel,
        shape((packed_rows + SLOT, 2 * local_rank), BF16),
        [(pos, SMEM), (total, VMEM), (packed_other, VMEM), (down, VMEM)],
        name="shrink_rest",
    )
    shrunk_other = lax.ppermute(shrunk, "narrow", by_y)
    slices, w_query, w_kv, _ = barrier((slices, w_query, w_kv, shrunk))
    q_c, kv_c = plane(w_query, by_c), plane(w_kv, by_c)
    s3 = rotate_z(slices[3], 3)
    shrunk_other, kv_x = barrier((shrunk_other, kv_x))
    slices = [slices[0], s1, s2]
    pieces = call(
        expand_kernel,
        [shape((SLOT, delta_cols), BF16)] * (2 * PLANE)
        + [shape((2 * SLOT, delta_cols), BF16)] * PLANE,
        [
            (pos, SMEM),
            (shrunk, VMEM),
            (shrunk_other, VMEM),
            (select, VMEM),
            (adapter_up_query[0], VMEM),
            (adapter_up_value[0], VMEM),
        ],
        name="expand",
    )

    def over_plane(four):
        return [four[0]] + [
            plane(four[i], perm) for i, perm in ((1, by_c), (2, by_x), (3, by_xc))
        ]

    first = over_plane(pieces[:PLANE])
    slices, kv_x, s3, _ = barrier((slices, kv_x, s3, pieces))
    slices = slices + [s3]
    kv_xc = plane(kv_x, by_c)
    padded = -(-height // SLOT) * SLOT
    base_a, base_b, owners = call(
        partial_kernel,
        [shape((nz, height, chunk_cols), F32)] * 2 + [shape((nz, 8, 128), BF16)],
        [(pos, SMEM), (inverse, SMEM)]
        + [(s, VMEM) for s in slices]
        + [(w, VMEM) for w in (w_query, q_c, q_x, q_xc, w_kv, kv_c, kv_x, kv_xc)],
        flops=2 * nz * height * width // nz * cols,
        nbytes=16 * 2**20,
        scratch=[pltpu.VMEM((nz * sliced, width // nz), BF16)],
        name="partial",
    )
    block = shape((height, chunk_cols), BF16)
    wide_block = shape((height, chunk_cols), F32)
    bases = [(pos, SMEM), (base_a, VMEM), (base_b, VMEM), (owners, VMEM)]

    def of(four):
        return [(p, VMEM) for p in four]

    sent = call(
        functools.partial(fill_kernel, 0), [block, block], bases + of(first), name="reduce_first"
    )
    received = [lax.ppermute(s, "z", INWARD) for s in sent]
    pieces, _ = barrier((pieces, sent))
    next_ = over_plane(pieces[PLANE : 2 * PLANE])
    rest = over_plane(pieces[2 * PLANE :])
    second = call(
        functools.partial(fill_kernel, 1), [wide_block] * 2, bases + of(next_), name="reduce_next"
    )
    received[0], rest = barrier((received[0], rest))
    *third, own_a, own_b = call(rest_kernel, [wide_block] * 4, bases + of(rest), name="reduce_rest")
    scalars = [(pos, SMEM), (table, SMEM)]
    ends, middles = [], []
    for chunk in range(2):
        out = call(
            second_kernel,
            block,
            scalars + of([sent[chunk], second[chunk], received[chunk]]),
            name="reduce_second",
        )
        middles.append(lax.ppermute(out, "z", MIDDLE))
        ends.append(lax.ppermute(out, "z", INWARD))
    for chunk in range(2):
        inner, outer = call(
            third_kernel,
            [block, block],
            of([second[chunk], third[chunk], ends[chunk], middles[chunk]]),
            name="reduce_third",
        )
        middles[chunk] = lax.ppermute(inner, "z", MIDDLE)
        ends[chunk] = lax.ppermute(outer, "z", PAIRS)

    angles = np.arange(REQ_LEN)[:, None] * (rope_theta ** (-np.arange(HD // 2) * (2.0 / HD)))[None, :]
    cosine = np.tile(np.concatenate([np.cos(angles)] * 2, axis=1), (requests_here, 1))
    sine = np.tile(np.concatenate([-np.sin(angles), np.sin(angles)], axis=1), (requests_here, 1))
    tables = [(jnp.asarray(a.astype(np.float32)), VMEM) for a in (cosine, sine)]
    near_cols = query_cols - chunk_cols
    group_rows = query_cols // key_cols * padded
    key_heads = key_cols // HD
    held = shape((key_heads, HD, HD), BF16)
    mask = shape((group_rows, HD), F32)
    near = call(
        attend_near_kernel,
        [shape((height, near_cols), BF16), held, held, mask, mask],
        [(request_tokens, SMEM)] + of([own_b, ends[1], middles[1]]) + tables,
        nbytes=8 * 2**20,
        scratch=[pltpu.VMEM((height, chunk_cols), F32), pltpu.VMEM((group_rows, HD), BF16)],
        name="attend_near",
    )
    return call(
        attend_kernel,
        shape((height, query_cols), BF16),
        of([own_a, ends[0], middles[0], *near]) + tables,
        scratch=[
            pltpu.VMEM((height, chunk_cols), F32),
            pltpu.VMEM((key_heads - 1, group_rows, HD), BF16),
        ],
        name="attend",
    )


def solution(mesh):
    wide, narrow = mesh.shape["wide"], mesh.shape["narrow"]
    if wide == 4 * PLANE and narrow == 2:
        grid = Mesh(mesh.devices.reshape(wide // PLANE, PLANE, narrow), ("z", "plane", "narrow"))
        body, on, over = reduce_body, grid, ("z", "plane")
    else:
        body, on, over = gather_body, mesh, "wide"
    return jax.shard_map(
        body,
        mesh=on,
        in_specs=(
            P(over, None),
            P(over, "narrow"),
            P(over, None, "narrow"),
            P(over, None, None, "narrow"),
            P(over, None, "narrow"),
            P(over, None, "narrow"),
            P(over),
            P(over),
            P(),
        ),
        out_specs=P(over, "narrow"),
        check_vma=False,
    )
```
